32 devices in a mesh: rows: 4 (over x, core), mp: 8 (over z, y).
Axes of the slice: x: 2, y: 2, z: 4, core: 2. Of those that a mesh axis runs over, the one named last changes fastest.
Arguments:
- inputs: bfloat16 [3, 512, 2304], P(None, 'rows', 'mp'), may hold values from -6 to 6
- gate_up: bfloat16 [3, 2304, 2, 9216], P(None, None, None, 'mp'), may hold values from -0.125 to 0.125
- down_weight: bfloat16 [3, 9216, 2304], P(None, 'mp'), may hold values from -0.09375 to 0.09375
- enc_weight: bfloat16 [3, 2304, 16384], P(None, None, 'mp'), may hold values from -0.125 to 0.125
- enc_bias: float32 [3, 16384], P(None, 'mp'), may hold values from -3 to 3
- dec_weight: bfloat16 [6, 16384, 2304], P(None, 'mp', 'rows'), may hold values from -0.09375 to 0.09375
Outputs:
- recon: float32 [3, 512, 2304], P(None, 'rows', 'mp')
- residual: float32 [3, 512, 2304], P(None, 'rows', 'mp')
The draws below stay inside these ranges and needn't reach their ends.
All inputs are finite; a program needn't handle non-finite values.
Results may differ from the reference program's by a relative error of at most 0.0029.
Values may be sent and summed in bfloat16 or wider, within the bound.
A program may use at most 256 MiB of HBM per device.

```python
import jax
import jax.numpy as jnp

D = 2304
FF = 9216
LAT = 16384
LAYERS = 3
PAIRS = 6
TOKENS = 512


def strengthened(values, own_key, source, target, parts, factor):
    owner, partner = [(jnp.arange(values.shape[dim]) // (values.shape[dim] // parts)).reshape([-1 if axis == dim else 1 for axis in range(values.ndim)]) for dim in (source, target)]
    chosen = jax.random.permutation(own_key, parts)[partner]
    strong = (owner == chosen) | (owner == (partner + parts // 2) % parts)
    return jnp.where(strong, factor * values, values)


def block_scale(key, shape, shards, low, largest):
    factor_of = 1.0
    for position, shards_of in shards:
        steps = jax.random.uniform(jax.random.fold_in(jax.random.fold_in(key, 6), position), (shards_of,), jnp.float32, low / len(shards), largest / len(shards))
        factor_of = factor_of * jnp.repeat(jnp.exp(steps), shape[position] // shards_of).reshape((-1,) + (1,) * (len(shape) - 1 - position))
    return factor_of


def normal_values(rng, shape, width, reach, split=(), dtype=jnp.bfloat16):
    array = jax.random.normal(rng, shape, jnp.float32) * width
    if len(split) > 0:
        array = block_scale(rng, shape, split, -0.22, 0.18) * array
    return jnp.clip(array, min=-reach, max=reach).astype(dtype)


def gaussian_with(own_key, extent, deviation, reach, cuts, heavy, held_as=jnp.bfloat16):
    array = deviation * jax.random.normal(own_key, extent, jnp.float32)
    if cuts:
        array = array * block_scale(own_key, extent, cuts, -0.22, 0.18)
    return jnp.clip(strengthened(array, jax.random.fold_in(own_key, 3), *heavy), -reach, reach).astype(held_as)


def setup_inputs(seed: int = 0) -> dict:
    key_list = jax.random.split(jax.random.key(seed), 7)
    inputs = normal_values(key_list[0], (LAYERS, TOKENS, D), 1.0, 6.0, ((1, 4), (2, 8)))
    gate_up = normal_values(key_list[1], (LAYERS, D, 2, FF), D ** -0.5, 0.125, ((3, 8),))
    down_weight = gaussian_with(key_list[2], (LAYERS, FF, D), FF ** -0.5, 0.09375, ((1, 8),), (1, 2, 8, 2.0))
    enc_weight = normal_values(key_list[3], (LAYERS, D, LAT), D ** -0.5, 0.125, ((2, 8),))
    enc_bias = normal_values(key_list[4], (LAYERS, LAT), 0.5, 3.0, ((1, 8),), jnp.float32)
    dec_weight = gaussian_with(key_list[5], (PAIRS, LAT, D), (LAT // 2) ** -0.5, 0.09375, ((1, 8), (2, 4)), (1, 2, 8, 2.0))
    return {"inputs": inputs, "gate_up": gate_up, "down_weight": down_weight, "enc_weight": enc_weight, "enc_bias": enc_bias, "dec_weight": dec_weight}


def reference(inputs, gate_up, down_weight, enc_weight, enc_bias, dec_weight):
    targets = []
    latents = []
    for layer in range(LAYERS):
        rows_in = inputs[layer]
        gate = jnp.dot(rows_in, gate_up[layer, :, 0, :], preferred_element_type=jnp.float32)
        upper = jnp.dot(rows_in, gate_up[layer, :, 1, :], preferred_element_type=jnp.float32)
        hidden = (jax.nn.gelu(gate, approximate=True) * upper).astype(jnp.bfloat16)
        targets.append(jnp.dot(hidden, down_weight[layer], preferred_element_type=jnp.float32))
        pre_act = jnp.dot(rows_in, enc_weight[layer], preferred_element_type=jnp.float32) + enc_bias[layer][None, :]
        latents.append(jax.nn.relu(pre_act).astype(jnp.bfloat16))
    recons = []
    for target_layer in range(LAYERS):
        total = jnp.zeros((TOKENS, D), jnp.float32)
        for source in range(target_layer + 1):
            pair = target_layer * (target_layer + 1) // 2 + source
            total = total + jnp.dot(latents[source], dec_weight[pair], preferred_element_type=jnp.float32)
        recons.append(total)
    recon = jnp.stack(recons)
    residual = jnp.stack(targets) - recon
    return recon, residual
```

```python
import jax
import jax.numpy as jnp
from jax import lax
from jax.sharding import PartitionSpec as P


def flip_permutation(count):
    return [(index, index ^ 1) for index in range(count)]


def shift_permutation(count, inner, distance):
    outer = count // inner
    return [
        (index, ((index // inner + distance) % outer) * inner + index % inner)
        for index in range(count)
    ]


def gather_inputs(rows_in, me, count):
    outer = count // 2
    position, parity = me // 2, me % 2
    parts = [rows_in] + [
        lax.ppermute(rows_in, "mp", shift_permutation(count, 2, distance))
        for distance in range(1, outer)
    ]
    around = jnp.stack([parts[(-index) % outer] for index in range(2 * outer - 1)])
    mine = lax.dynamic_slice_in_dim(around, (outer - position) % outer, outer, 0)
    other = lax.ppermute(mine, "mp", flip_permutation(count))
    even = jnp.where(parity == 0, mine, other)
    odd = jnp.where(parity == 0, other, mine)
    both = jnp.stack([even, odd], axis=1)
    rows, width = rows_in.shape
    return both.transpose(2, 0, 1, 3).reshape(rows, count * width)


def gather_rows(latent, me, count):
    outer = count // 2
    position, parity = me // 2, me % 2
    parts = [latent] + [
        lax.ppermute(latent, "rows", shift_permutation(count, 2, distance))
        for distance in range(1, outer)
    ]
    around = jnp.stack([parts[(-index) % outer] for index in range(2 * outer - 1)])
    mine = lax.dynamic_slice_in_dim(around, (outer - position) % outer, outer, 0)
    other = lax.ppermute(mine, "rows", flip_permutation(count))
    even = jnp.where(parity == 0, mine, other)
    odd = jnp.where(parity == 0, other, mine)
    both = jnp.stack([even, odd], axis=1)
    return both.reshape(count * latent.shape[0], latent.shape[1])


def scatter_sum(pieces, me, count):
    outer = count // 2
    position, parity = me // 2, me % 2
    split = pieces.reshape((outer, 2) + pieces.shape[1:])
    sent = jnp.where(parity == 0, split[:, 1], split[:, 0]).astype(jnp.bfloat16)
    kept = jnp.where(parity == 0, split[:, 0], split[:, 1])
    arrived = lax.ppermute(sent, "mp", flip_permutation(count))
    summed = kept + arrived.astype(jnp.float32)
    total = lax.dynamic_index_in_dim(summed, position, 0, keepdims=False)
    narrow = summed.astype(jnp.bfloat16)
    for distance in range(1, outer):
        block = lax.dynamic_index_in_dim(
            narrow, (position + distance) % outer, 0, keepdims=False
        )
        arrived = lax.ppermute(block, "mp", shift_permutation(count, 2, distance))
        total = total + arrived.astype(jnp.float32)
    return total


def body(inputs, gate_up, down_weight, enc_weight, enc_bias, dec_weight):
    layers, rows, width = inputs.shape
    model_width = gate_up.shape[1]
    hidden_local = gate_up.shape[3]
    across, count = lax.axis_size("rows"), lax.axis_size("mp")
    my_row, me = lax.axis_index("rows"), lax.axis_index("mp")
    blocks = count // across

    gathered = [gather_inputs(inputs[layer], me, count) for layer in range(layers)]
    latents = []
    for layer in range(layers):
        pre = jnp.dot(gathered[layer], enc_weight[layer], preferred_element_type=jnp.float32)
        latent = jax.nn.relu(pre + enc_bias[layer][None, :]).astype(jnp.bfloat16)
        latents.append(gather_rows(latent, my_row, across))
    targets = []
    for layer in range(layers):
        joined = gate_up[layer].reshape(model_width, 2 * hidden_local)
        pre = jnp.dot(gathered[layer], joined, preferred_element_type=jnp.float32)
        gate, upper = pre[:, :hidden_local], pre[:, hidden_local:]
        hidden = (jax.nn.gelu(gate, approximate=True) * upper).astype(jnp.bfloat16)
        partial = jnp.dot(hidden, down_weight[layer], preferred_element_type=jnp.float32)
        pieces = partial.reshape(rows, count, width).transpose(1, 0, 2)
        targets.append(scatter_sum(pieces, me, count))
    home = [
        (r * count + a * blocks + c, a * count + r * blocks + c)
        for r in range(across)
        for a in range(across)
        for c in range(blocks)
    ]
    recons = []
    for target in range(layers):
        partial = sum(
            jnp.dot(
                latents[source],
                dec_weight[target * (target + 1) // 2 + source],
                preferred_element_type=jnp.float32,
            )
            for source in range(target + 1)
        )
        pieces = partial.reshape(across, rows, blocks, width).transpose(0, 2, 1, 3)
        summed = scatter_sum(pieces.reshape(count, rows, width), me, count)
        recons.append(lax.ppermute(summed, ("rows", "mp"), home))
    recon = jnp.stack(recons)
    residual = jnp.stack(targets) - recon
    return (recon, residual)


def solution(mesh):
    in_specs = (
        P(None, "rows", "mp"),
        P(None, None, None, "mp"),
        P(None, "mp", None),
        P(None, None, "mp"),
        P(None, "mp"),
        P(None, "mp", "rows"),
    )
    out_specs = (P(None, "rows", "mp"), P(None, "rows", "mp"))
    return jax.shard_map(body, mesh=mesh, in_specs=in_specs, out_specs=out_specs, check_vma=False)
```

```python
import functools

import jax
import jax.numpy as jnp
from jax import lax
from jax.experimental import pallas as pl
from jax.experimental.pallas import tpu as pltpu
from jax.sharding import PartitionSpec as P


def flip_permutation(count):
    return [(index, index ^ 1) for index in range(count)]


def shift_permutation(count, inner, distance):
    outer = count // inner
    return [
        (index, ((index // inner + distance) % outer) * inner + index % inner)
        for index in range(count)
    ]


def gather_inputs(rows_in, me, count):
    outer = count // 2
    position, parity = me // 2, me % 2
    parts = [rows_in] + [
        lax.ppermute(rows_in, "mp", shift_permutation(count, 2, distance))
        for distance in range(1, outer)
    ]
    around = jnp.stack([parts[(-index) % outer] for index in range(2 * outer - 1)])
    mine = lax.dynamic_slice_in_dim(around, (outer - position) % outer, outer, 0)
    other = lax.ppermute(mine, "mp", flip_permutation(count))
    even = jnp.where(parity == 0, mine, other)
    odd = jnp.where(parity == 0, other, mine)
    both = jnp.stack([even, odd], axis=1)
    rows, width = rows_in.shape
    return both.transpose(2, 0, 1, 3).reshape(rows, count * width)


def gather_rows(latent, me, count):
    outer = count // 2
    position, parity = me // 2, me % 2
    parts = [latent] + [
        lax.ppermute(latent, "rows", shift_permutation(count, 2, distance))
        for distance in range(1, outer)
    ]
    around = jnp.stack([parts[(-index) % outer] for index in range(2 * outer - 1)])
    mine = lax.dynamic_slice_in_dim(around, (outer - position) % outer, outer, 0)
    other = lax.ppermute(mine, "rows", flip_permutation(count))
    even = jnp.where(parity == 0, mine, other)
    odd = jnp.where(parity == 0, other, mine)
    both = jnp.stack([even, odd], axis=1)
    return both.reshape(count * latent.shape[0], latent.shape[1])


def scatter_sum(pieces, me, count):
    outer = count // 2
    position, parity = me // 2, me % 2
    split = pieces.reshape((outer, 2) + pieces.shape[1:])
    sent = jnp.where(parity == 0, split[:, 1], split[:, 0]).astype(jnp.bfloat16)
    kept = jnp.where(parity == 0, split[:, 0], split[:, 1])
    arrived = lax.ppermute(sent, "mp", flip_permutation(count))
    summed = kept + arrived.astype(jnp.float32)
    total = lax.dynamic_index_in_dim(summed, position, 0, keepdims=False)
    narrow = summed.astype(jnp.bfloat16)
    for distance in range(1, outer):
        block = lax.dynamic_index_in_dim(
            narrow, (position + distance) % outer, 0, keepdims=False
        )
        arrived = lax.ppermute(block, "mp", shift_permutation(count, 2, distance))
        total = total + arrived.astype(jnp.float32)
    return total


def hidden_kernel(spread_ref, weight_ref, hidden_ref, total_ref):
    step = pl.program_id(0)
    depth, _, columns = weight_ref.shape[1:]

    @pl.when(step == 0)
    def _():
        total_ref[...] = jnp.zeros_like(total_ref)

    weight = weight_ref[0].reshape(2 * depth, columns)
    total_ref[...] += jnp.dot(spread_ref[...], weight, preferred_element_type=jnp.float32)

    @pl.when(step == pl.num_programs(0) - 1)
    def _():
        rows = hidden_ref.shape[0]
        gate, upper = total_ref[:rows], total_ref[rows:]
        hidden = jax.nn.gelu(gate, approximate=True) * upper
        hidden_ref[...] = hidden.astype(hidden_ref.dtype)


def hidden_units(rows_in, gate_up, layer):
    rows, model_width = rows_in.shape
    hidden_local = gate_up.shape[3]
    depth = max(d for d in range(128, 385, 128) if model_width % d == 0)
    zeros = jnp.zeros_like(rows_in)
    spread = jnp.concatenate(
        [jnp.stack([rows_in, zeros], axis=2), jnp.stack([zeros, rows_in], axis=2)]
    ).reshape(2 * rows, 2 * model_width)
    return pl.pallas_call(
        hidden_kernel,
        grid=(model_width // depth,),
        in_specs=[
            pl.BlockSpec((2 * rows, 2 * depth), lambda step: (0, step)),
            pl.BlockSpec((1, depth, 2, hidden_local), lambda step: (layer, step, 0, 0)),
        ],
        out_specs=pl.BlockSpec((rows, hidden_local), lambda step: (0, 0)),
        out_shape=jax.ShapeDtypeStruct((rows, hidden_local), jnp.bfloat16),
        scratch_shapes=[pltpu.VMEM((2 * rows, hidden_local), jnp.float32)],
        cost_estimate=pl.CostEstimate(
            flops=8 * rows * model_width * hidden_local,
            bytes_accessed=4 * model_width * hidden_local,
            transcendentals=rows * hidden_local,
        ),
        compiler_params=pltpu.CompilerParams(vmem_limit_bytes=24 * 1024 * 1024),
    )(spread, gate_up)


def body(inputs, gate_up, down_weight, enc_weight, enc_bias, dec_weight):
    layers, rows, width = inputs.shape
    across, count = lax.axis_size("rows"), lax.axis_size("mp")
    my_row, me = lax.axis_index("rows"), lax.axis_index("mp")
    blocks = count // across

    gathered = [gather_inputs(inputs[layer], me, count) for layer in range(layers)]
    latents = []
    for layer in range(layers):
        pre = jnp.dot(gathered[layer], enc_weight[layer], preferred_element_type=jnp.float32)
        latent = jax.nn.relu(pre + enc_bias[layer][None, :]).astype(jnp.bfloat16)
        latents.append(gather_rows(latent, my_row, across))
    targets = []
    for layer in range(layers):
        hidden = hidden_units(gathered[layer], gate_up, layer)
        partial = jnp.dot(hidden, down_weight[layer], preferred_element_type=jnp.float32)
        partial = lax.optimization_barrier(partial)
        pieces = partial.reshape(rows, count, width).transpose(1, 0, 2)
        targets.append(scatter_sum(pieces, me, count))
    home = [
        (r * count + a * blocks + c, a * count + r * blocks + c)
        for r in range(across)
        for a in range(across)
        for c in range(blocks)
    ]
    recons = []
    for target in range(layers):
        partial = sum(
            jnp.dot(
                latents[source],
                dec_weight[target * (target + 1) // 2 + source],
                preferred_element_type=jnp.float32,
            )
            for source in range(target + 1)
        )
        pieces = partial.reshape(across, rows, blocks, width).transpose(0, 2, 1, 3)
        summed = scatter_sum(pieces.reshape(count, rows, width), me, count)
        recons.append(lax.ppermute(summed, ("rows", "mp"), home))
    recon = jnp.stack(recons)
    residual = jnp.stack(targets) - recon
    return (recon, residual)


def solution(mesh):
    in_specs = (
        P(None, "rows", "mp"),
        P(None, None, None, "mp"),
        P(None, "mp", None),
        P(None, None, "mp"),
        P(None, "mp"),
        P(None, "mp", "rows"),
    )
    out_specs = (P(None, "rows", "mp"), P(None, "rows", "mp"))
    return jax.shard_map(body, mesh=mesh, in_specs=in_specs, out_specs=out_specs, check_vma=False)
```

```python
import functools

import jax
import jax.numpy as jnp
from jax import lax
from jax.experimental import pallas as pl
from jax.experimental.pallas import tpu as pltpu
from jax.sharding import PartitionSpec as P


def flip_permutation(count):
    return [(index, index ^ 1) for index in range(count)]


def shift_permutation(count, inner, distance):
    outer = count // inner
    return [
        (index, ((index // inner + distance) % outer) * inner + index % inner)
        for index in range(count)
    ]


def gather_inputs(rows_in, me, count):
    outer = count // 2
    position, parity = lax.div(me, 2), lax.rem(me, 2)
    parts = [rows_in] + [
        lax.ppermute(rows_in, "mp", shift_permutation(count, 2, distance))
        for distance in range(1, outer)
    ]
    around = jnp.stack([parts[(-index) % outer] for index in range(2 * outer - 1)])
    mine = lax.dynamic_slice_in_dim(around, lax.rem(outer - position, outer), outer, 0)
    other = lax.ppermute(mine, "mp", flip_permutation(count))
    even = jnp.where(parity == 0, mine, other)
    odd = jnp.where(parity == 0, other, mine)
    both = jnp.stack([even, odd], axis=1)
    chunk, rows, width = rows_in.shape
    both = both.transpose(2, 3, 0, 1, 4).reshape(chunk, rows, count * width)
    return [both[index] for index in range(chunk)]


def gather_rows(latent, me, count):
    outer = count // 2
    position, parity = lax.div(me, 2), lax.rem(me, 2)
    parts = [latent] + [
        lax.ppermute(latent, "rows", shift_permutation(count, 2, distance))
        for distance in range(1, outer)
    ]
    around = jnp.stack([parts[(-index) % outer] for index in range(2 * outer - 1)])
    mine = lax.dynamic_slice_in_dim(around, lax.rem(outer - position, outer), outer, 0)
    other = lax.ppermute(mine, "rows", flip_permutation(count))
    even = jnp.where(parity == 0, mine, other)
    odd = jnp.where(parity == 0, other, mine)
    both = jnp.stack([even, odd], axis=1)
    return both.reshape(count * latent.shape[0], latent.shape[1])


def scatter_sum(pieces, me, count):
    outer = count // 2
    position, parity = lax.div(me, 2), lax.rem(me, 2)
    split = pieces.reshape((outer, 2) + pieces.shape[1:])
    sent = jnp.where(parity == 0, split[:, 1], split[:, 0]).astype(jnp.bfloat16)
    kept = jnp.where(parity == 0, split[:, 0], split[:, 1])
    arrived = lax.ppermute(sent, "mp", flip_permutation(count))
    summed = kept + arrived.astype(jnp.float32)
    total = lax.dynamic_index_in_dim(summed, position, 0, keepdims=False)
    narrow = summed.astype(jnp.bfloat16)
    for distance in range(1, outer):
        block = lax.dynamic_index_in_dim(
            narrow, lax.rem(position + distance, outer), 0, keepdims=False
        )
        arrived = lax.ppermute(block, "mp", shift_permutation(count, 2, distance))
        total = total + arrived.astype(jnp.float32)
    return total


def hidden_kernel(rows_ref, weight_ref, hidden_ref, total_ref):
    step = pl.program_id(0)
    depth, _, columns = weight_ref.shape[1:]

    @pl.when(step == 0)
    def _():
        total_ref[...] = jnp.zeros_like(total_ref)

    weight = weight_ref[0].reshape(2 * depth, columns)
    rows_in = rows_ref[...]
    place = lax.broadcasted_iota(jnp.int32, (depth, 2 * depth), 1)
    place = place - 2 * lax.broadcasted_iota(jnp.int32, (depth, 2 * depth), 0)
    spread = jnp.concatenate(
        [
            jnp.dot(
                rows_in,
                jnp.where(place == kind, 1.0, 0.0).astype(rows_in.dtype),
                preferred_element_type=jnp.float32,
            ).astype(rows_in.dtype)
            for kind in range(2)
        ]
    )
    total_ref[...] += jnp.dot(spread, weight, preferred_element_type=jnp.float32)

    @pl.when(step == pl.num_programs(0) - 1)
    def _():
        rows = hidden_ref.shape[0]
        gate, upper = total_ref[:rows], total_ref[rows:]
        hidden = jax.nn.gelu(gate, approximate=True) * upper
        hidden_ref[...] = hidden.astype(hidden_ref.dtype)


def hidden_units(rows_in, gate_up, layer):
    rows, model_width = rows_in.shape
    hidden_local = gate_up.shape[3]
    depth = max(d for d in range(128, 385, 128) if model_width % d == 0)
    return pl.pallas_call(
        hidden_kernel,
        grid=(model_width // depth,),
        in_specs=[
            pl.BlockSpec((rows, depth), lambda step: (0, step)),
            pl.BlockSpec((1, depth, 2, hidden_local), lambda step: (layer, step, 0, 0)),
        ],
        out_specs=pl.BlockSpec((rows, hidden_local), lambda step: (0, 0)),
        out_shape=jax.ShapeDtypeStruct((rows, hidden_local), jnp.bfloat16),
        scratch_shapes=[pltpu.VMEM((2 * rows, hidden_local), jnp.float32)],
        cost_estimate=pl.CostEstimate(
            flops=8 * rows * model_width * hidden_local,
            bytes_accessed=4 * model_width * hidden_local,
            transcendentals=rows * hidden_local,
        ),
        compiler_params=pltpu.CompilerParams(vmem_limit_bytes=24 * 1024 * 1024),
    )(rows_in, gate_up)


def body(inputs, gate_up, down_weight, enc_weight, enc_bias, dec_weight):
    layers, rows, width = inputs.shape
    across, count = lax.axis_size("rows"), lax.axis_size("mp")
    my_row, me = lax.axis_index("rows"), lax.axis_index("mp")
    blocks = count // across

    gathered = gather_inputs(inputs[:1], me, count) + gather_inputs(inputs[1:], me, count)
    local = []
    for layer in range(layers):
        pre = jnp.dot(gathered[layer], enc_weight[layer], preferred_element_type=jnp.float32)
        local.append(jax.nn.relu(pre + enc_bias[layer][None, :]).astype(jnp.bfloat16))
    gathered, local = lax.optimization_barrier((gathered, local))
    latents = [gather_rows(latent, my_row, across) for latent in local]
    chunks = [range(layers - 1), range(layers - 1, layers)]
    targets = []
    for chunk in chunks:
        pieces = []
        for layer in chunk:
            hidden = hidden_units(gathered[layer], gate_up, layer)
            partial = jnp.dot(hidden, down_weight[layer], preferred_element_type=jnp.float32)
            partial = lax.optimization_barrier(partial)
            pieces.append(partial.reshape(rows, count, width).transpose(1, 0, 2))
        targets.append(scatter_sum(jnp.stack(pieces, axis=1), me, count))
    home = [
        (r * count + a * blocks + c, a * count + r * blocks + c)
        for r in range(across)
        for a in range(across)
        for c in range(blocks)
    ]
    recons = []
    for chunk in chunks:
        pieces = []
        for target in chunk:
            partial = sum(
                jnp.dot(
                    latents[source],
                    dec_weight[target * (target + 1) // 2 + source],
                    preferred_element_type=jnp.float32,
                )
                for source in range(target + 1)
            )
            blocked = partial.reshape(across, rows, blocks, width).transpose(0, 2, 1, 3)
            pieces.append(blocked.reshape(count, rows, width))
        summed = scatter_sum(jnp.stack(pieces, axis=1), me, count)
        recons.append(lax.ppermute(summed, ("rows", "mp"), home))
    recon = jnp.concatenate(recons)
    residual = jnp.concatenate(targets) - recon
    return (recon, residual)


def solution(mesh):
    in_specs = (
        P(None, "rows", "mp"),
        P(None, None, None, "mp"),
        P(None, "mp", None),
        P(None, None, "mp"),
        P(None, "mp"),
        P(None, "mp", "rows"),
    )
    out_specs = (P(None, "rows", "mp"), P(None, "rows", "mp"))
    return jax.shard_map(body, mesh=mesh, in_specs=in_specs, out_specs=out_specs, check_vma=False)
```

```python
import functools

import jax
import jax.numpy as jnp
from jax import lax
from jax.experimental import pallas as pl
from jax.experimental.pallas import tpu as pltpu
from jax.sharding import PartitionSpec as P


def flip_permutation(count):
    return [(index, index ^ 1) for index in range(count)]


def shift_permutation(count, inner, distance):
    outer = count // inner
    return [
        (index, ((index // inner + distance) % outer) * inner + index % inner)
        for index in range(count)
    ]


def gather_inputs(rows_in, me, count):
    outer = count // 2
    position, parity = lax.div(me, 2), lax.rem(me, 2)
    parts = [rows_in] + [
        lax.ppermute(rows_in, "mp", shift_permutation(count, 2, distance))
        for distance in range(1, outer)
    ]
    around = jnp.stack([parts[(-index) % outer] for index in range(2 * outer - 1)])
    mine = lax.dynamic_slice_in_dim(around, lax.rem(outer - position, outer), outer, 0)
    other = lax.ppermute(mine, "mp", flip_permutation(count))
    even = jnp.where(parity == 0, mine, other)
    odd = jnp.where(parity == 0, other, mine)
    both = jnp.stack([even, odd], axis=1)
    chunk, rows, width = rows_in.shape
    both = both.transpose(2, 3, 0, 1, 4).reshape(chunk, rows, count * width)
    return [both[index] for index in range(chunk)]


def gather_rows(latent, me, count):
    outer = count // 2
    position, parity = lax.div(me, 2), lax.rem(me, 2)
    parts = [latent] + [
        lax.ppermute(latent, "rows", shift_permutation(count, 2, distance))
        for distance in range(1, outer)
    ]
    around = jnp.stack([parts[(-index) % outer] for index in range(2 * outer - 1)])
    mine = lax.dynamic_slice_in_dim(around, lax.rem(outer - position, outer), outer, 0)
    other = lax.ppermute(mine, "rows", flip_permutation(count))
    even = jnp.where(parity == 0, mine, other)
    odd = jnp.where(parity == 0, other, mine)
    both = jnp.stack([even, odd], axis=1)
    layers, rows, width = latent.shape
    return [both[:, :, layer].reshape(count * rows, width) for layer in range(layers)]


def scatter_sum(pieces, me, count):
    outer = count // 2
    position, parity = lax.div(me, 2), lax.rem(me, 2)
    split = pieces.reshape((outer, 2) + pieces.shape[1:])
    sent = jnp.where(parity == 0, split[:, 1], split[:, 0]).astype(jnp.bfloat16)
    kept = jnp.where(parity == 0, split[:, 0], split[:, 1])
    arrived = lax.ppermute(sent, "mp", flip_permutation(count))
    summed = kept + arrived.astype(jnp.float32)
    total = lax.dynamic_index_in_dim(summed, position, 0, keepdims=False)
    narrow = summed.astype(jnp.bfloat16)
    for distance in range(1, outer):
        block = lax.dynamic_index_in_dim(
            narrow, lax.rem(position + distance, outer), 0, keepdims=False
        )
        arrived = lax.ppermute(block, "mp", shift_permutation(count, 2, distance))
        total = total + arrived.astype(jnp.float32)
    return total


def hidden_kernel(rows_ref, weight_ref, hidden_ref, total_ref):
    step = pl.program_id(0)
    depth, _, columns = weight_ref.shape[1:]

    @pl.when(step == 0)
    def _():
        total_ref[...] = jnp.zeros_like(total_ref)

    weight = weight_ref[0].reshape(2 * depth, columns)
    rows_in = rows_ref[...]
    place = lax.broadcasted_iota(jnp.int32, (depth, 2 * depth), 1)
    place = place - 2 * lax.broadcasted_iota(jnp.int32, (depth, 2 * depth), 0)
    spread = jnp.concatenate(
        [
            jnp.dot(
                rows_in,
                jnp.where(place == kind, 1.0, 0.0).astype(rows_in.dtype),
                preferred_element_type=jnp.float32,
            ).astype(rows_in.dtype)
            for kind in range(2)
        ]
    )
    total_ref[...] += jnp.dot(spread, weight, preferred_element_type=jnp.float32)

    @pl.when(step == pl.num_programs(0) - 1)
    def _():
        rows = hidden_ref.shape[0]
        gate, upper = total_ref[:rows], total_ref[rows:]
        hidden = jax.nn.gelu(gate, approximate=True) * upper
        hidden_ref[...] = hidden.astype(hidden_ref.dtype)


def hidden_units(rows_in, gate_up, layer):
    rows, model_width = rows_in.shape
    hidden_local = gate_up.shape[3]
    depth = max(d for d in range(128, 385, 128) if model_width % d == 0)
    return pl.pallas_call(
        hidden_kernel,
        grid=(model_width // depth,),
        in_specs=[
            pl.BlockSpec((rows, depth), lambda step: (0, step)),
            pl.BlockSpec((1, depth, 2, hidden_local), lambda step: (layer, step, 0, 0)),
        ],
        out_specs=pl.BlockSpec((rows, hidden_local), lambda step: (0, 0)),
        out_shape=jax.ShapeDtypeStruct((rows, hidden_local), jnp.bfloat16),
        scratch_shapes=[pltpu.VMEM((2 * rows, hidden_local), jnp.float32)],
        cost_estimate=pl.CostEstimate(
            flops=8 * rows * model_width * hidden_local,
            bytes_accessed=4 * model_width * hidden_local,
            transcendentals=rows * hidden_local,
        ),
        compiler_params=pltpu.CompilerParams(vmem_limit_bytes=24 * 1024 * 1024),
    )(rows_in, gate_up)


def body(inputs, gate_up, down_weight, enc_weight, enc_bias, dec_weight):
    layers, rows, width = inputs.shape
    across, count = lax.axis_size("rows"), lax.axis_size("mp")
    my_row, me = lax.axis_index("rows"), lax.axis_index("mp")
    blocks = count // across

    gathered = gather_inputs(inputs[:1], me, count) + gather_inputs(inputs[1:], me, count)
    local = []
    for layer in range(layers):
        pre = jnp.dot(gathered[layer], enc_weight[layer], preferred_element_type=jnp.float32)
        local.append(jax.nn.relu(pre + enc_bias[layer][None, :]).astype(jnp.bfloat16))
    gathered, local = lax.optimization_barrier((gathered, jnp.stack(local)))
    latents = gather_rows(local, my_row, across)
    chunks = [range(layers - 1), range(layers - 1, layers)]
    targets = []
    for chunk in chunks:
        pieces = []
        for layer in chunk:
            hidden = hidden_units(gathered[layer], gate_up, layer)
            partial = jnp.dot(hidden, down_weight[layer], preferred_element_type=jnp.float32)
            partial = lax.optimization_barrier(partial)
            pieces.append(partial.reshape(rows, count, width).transpose(1, 0, 2))
        targets.append(scatter_sum(jnp.stack(pieces, axis=1), me, count))
    home = [
        (r * count + a * blocks + c, a * count + r * blocks + c)
        for r in range(across)
        for a in range(across)
        for c in range(blocks)
    ]
    recons = []
    for chunk in chunks:
        pieces = []
        for target in chunk:
            partial = sum(
                jnp.dot(
                    latents[source],
                    dec_weight[target * (target + 1) // 2 + source],
                    preferred_element_type=jnp.float32,
                )
                for source in range(target + 1)
            )
            blocked = partial.reshape(across, rows, blocks, width).transpose(0, 2, 1, 3)
            pieces.append(blocked.reshape(count, rows, width))
        summed = scatter_sum(jnp.stack(pieces, axis=1), me, count)
        recons.append(lax.ppermute(summed, ("rows", "mp"), home))
    recon = jnp.concatenate(recons)
    residual = jnp.concatenate(targets) - recon
    return (recon, residual)


def solution(mesh):
    in_specs = (
        P(None, "rows", "mp"),
        P(None, None, None, "mp"),
        P(None, "mp", None),
        P(None, None, "mp"),
        P(None, "mp"),
        P(None, "mp", "rows"),
    )
    out_specs = (P(None, "rows", "mp"), P(None, "rows", "mp"))
    return jax.shard_map(body, mesh=mesh, in_specs=in_specs, out_specs=out_specs, check_vma=False)
```
